32 devices in a mesh: pole: 2 (over y), row: 4 (over x, core), col: 4 (over z).
Axes of the slice: x: 2, y: 2, z: 4, core: 2. Of those that a mesh axis runs over, the one named last changes fastest.
Arguments:
- inverse_block: bfloat16 [16, 8, 256, 256], P(('pole', 'row'), 'col'), parts along dimension 0, may hold values from -6 to 6
- lower_block: bfloat16 [16, 8, 256, 256], P(('pole', 'row'), 'col'), parts along dimension 0, may hold values from -0.1875 to 0.1875
- pattern: int32 [8, 8], P('row', 'col'), may hold values 0 or 1
- diag_inverse: float32 [16, 256, 256], P(('pole', 'col'), 'row'), parts along dimension 0, may hold values from -6 to 6
Outputs:
- inverse_lower: bfloat16 [16, 8, 256, 256], P(('pole', 'row'), 'col'), parts along dimension 0
- inverse_diagonal: float32 [16, 256, 256], P(('pole', 'col'), 'row'), parts along dimension 0
The draws below stay inside these ranges and needn't reach their ends.
There are 2 independent parts, one for each index of `pole`. The reference program is written for one: setup_inputs(seed, part) draws one part's arguments, and reference() takes and returns one part's arrays. A program takes and returns all parts, laid end to end along the dimension named above; an argument that names none is the same for every part. Nothing has to cross between parts.
All inputs are finite; a program needn't handle non-finite values. No bound on the sum of `pattern` on one device may be relied on, other than what follows from the above.
Results may differ from the reference program's by a relative error of at most 0.006.
Values may be sent and summed in bfloat16 or wider, within the bound.
No kernel may reach another device: no remote copies, remote signals or barrier semaphores. Data moves between devices by JAX's collectives and lax.ppermute only.
A program may use at most 64 MiB of HBM per device.

```python
import jax
import jax.numpy as jnp
from jax import lax

B = 256
S = 8
KN = 8


def touch_ends(values, stream_key, smallest, largest):
    place = [jax.random.randint(jax.random.fold_in(stream_key, axis), (), 0, length) for axis, length in enumerate(values.shape)]
    main_axis = values.shape.index(max(values.shape))
    neighbour = place[:main_axis] + [(place[main_axis] + 1) % values.shape[main_axis]] + place[main_axis + 1:]
    return values.at[tuple(place)].set(smallest).at[tuple(neighbour)].set(largest)


def block_scale(stream_key, dims, cuts, smallest, top_value):
    loudness, own = 1.0, jax.random.fold_in(stream_key, 6)
    for dim, shards_of in cuts:
        steps = jnp.exp(jax.random.uniform(jax.random.fold_in(own, dim), (shards_of,), jnp.float32, smallest / len(cuts), top_value / len(cuts)))
        loudness = loudness * jnp.repeat(steps, dims[dim] // shards_of).reshape([-1 if axis == dim else 1 for axis in range(len(dims))])
    return loudness


def centred(rng, extent, width, most, split=(), held_as=jnp.bfloat16):
    factor_of = block_scale(rng, extent, split, -0.22, 0.18) if split else 1.0
    result = jax.random.normal(rng, extent, jnp.float32) * width * factor_of
    return jnp.minimum(jnp.maximum(result, -most), most).astype(held_as)


def setup_inputs(seed: int = 0, part: int = 0) -> dict:
    key_of = jax.random.split(jax.random.key(seed), 5)
    own_keys = jax.random.split(jax.random.fold_in(key_of[4], part), 5)
    inverse_block = centred(own_keys[0], (S, S, B, B), 1.0, 6.0, ((0, 4), (1, 4)))
    lower_block = centred(own_keys[1], (S, KN, B, B), (S * B // 2) ** -0.5, 0.1875, ((0, 4), (1, 4)))
    pattern = touch_ends((jax.random.randint(key_of[2], (S, KN), 0, 2) < 1).astype(jnp.int32), jax.random.fold_in(key_of[2], 1), 0, 1)
    diag_inverse = centred(own_keys[3], (KN, B, B), 1.0, 6.0, ((0, 4), (1, 4)), jnp.float32)
    return dict(inverse_block=inverse_block, lower_block=lower_block, pattern=pattern, diag_inverse=diag_inverse)


def reference(inverse_block, lower_block, pattern, diag_inverse):
    keep_mask = pattern.astype(jnp.float32)[:, :, None, None]
    masked = (lower_block.astype(jnp.float32) * keep_mask).astype(jnp.bfloat16)
    masked_wide = masked.astype(jnp.float32)

    def block_row(inverse_row):
        return jnp.einsum("jab,jkbc->kac", inverse_row.astype(jnp.float32), masked_wide)

    totals = lax.map(block_row, inverse_block)
    inverse_lower = (-(keep_mask * totals)).astype(jnp.bfloat16)
    updates = jnp.einsum("ikba,ikbc->kac", masked_wide, inverse_lower.astype(jnp.float32))
    inverse_diagonal = diag_inverse - updates
    return inverse_lower, inverse_diagonal
```

```python
import functools

import jax
import jax.numpy as jnp
from jax import lax
from jax.experimental import pallas as pl
from jax.experimental.pallas import tpu as pltpu
from jax.sharding import PartitionSpec as P

F32, BF16 = jnp.float32, jnp.bfloat16
VMEM = pl.BlockSpec(memory_space=pltpu.VMEM)
SMEM = pl.BlockSpec(memory_space=pltpu.SMEM)


def link_pairs(n, parity, step):
    pairs = []
    for i in range(parity, n - 1, 2):
        if i - step >= 0:
            pairs.append((i, i + 1))
        if i + 1 + step <= n - 1:
            pairs.append((i + 1, i))
    return pairs


def line_gather(own, axis, n, spread):
    me = lax.axis_index(axis) // spread
    even = lax.rem(me, 2) == 0
    rounds = []
    via = [own, own]
    for step in range(n - 1):
        arrived = [None, None]
        got = []
        for parity in (0, 1):
            pairs = link_pairs(n, parity, step)
            if not pairs:
                continue
            wide = [(a * spread + c, b * spread + c) for a, b in pairs for c in range(spread)]
            arrived[parity] = lax.ppermute(via[parity], axis, wide)
            from_above = even if parity == 0 else jnp.logical_not(even)
            source = jnp.where(from_above, me + 1 + step, me - 1 - step)
            source = jnp.where((source >= 0) & (source < n), source, -1)
            got.append((arrived[parity], source))
        rounds.append(got)
        via = [arrived[1], arrived[0]]
    return rounds


def mask_kernel(pattern, lower, masked):
    rows, cols = lower.shape[:2]
    for j in range(rows):
        for k in range(cols):
            keep = pattern[j, k].astype(F32)
            masked[j, k] = (lower[j, k].astype(F32) * keep).astype(BF16)


def mask(pattern, lower):
    return pl.pallas_call(
        mask_kernel,
        out_shape=jax.ShapeDtypeStruct(lower.shape, BF16),
        in_specs=[SMEM, VMEM],
        out_specs=VMEM,
    )(pattern, lower)


def add_products(place, block, factor, total):
    @pl.when(place >= 0)
    def _():
        at = jnp.maximum(place, 0)
        rows, inner = block.shape[:2]
        for i in range(rows):
            for k in range(total.shape[1]):
                partial = total[i, k]
                for j in range(inner):
                    partial += jnp.dot(block[i, j], factor[at, j, k], preferred_element_type=F32)
                total[i, k] = partial


def partial_kernel(count, places, *refs):
    blocks, (factor, total) = refs[:count], refs[count:]
    total[...] = jnp.zeros_like(total)
    for n, block in enumerate(blocks):
        add_products(places[n], block, factor, total)


def finish_kernel(count, n_row, places, *refs):
    blocks, (factor, total_in, pattern, masked, lower_out), sends = (
        refs[:count], refs[count:count + 5], refs[count + 5:]
    )
    total = sends[-1]
    sends = sends[:-1]
    total[...] = total_in[...]
    for n, block in enumerate(blocks):
        add_products(places[n], block, factor, total)
    me = places[count]
    rows, cols, b = total.shape[:3]
    piece = b // n_row
    for k in range(cols):
        update = jnp.zeros((b, b), F32)
        for i in range(rows):
            keep = pattern[i, k].astype(F32)
            value = (-(keep * total[i, k])).astype(BF16)
            lower_out[i, k] = value
            update += lax.dot_general(
                masked[i, k], value, (((0,), (0,)), ((), ())), preferred_element_type=F32
            )
        total[0, k] = update
    for d in range(n_row):
        there = jnp.bitwise_xor(me, d)
        for k in range(cols):
            sends[d][k] = total[0, k, pl.ds(pl.multiple_of(there * piece, 16), piece), :].astype(sends[d].dtype)


def last_kernel(*refs):
    diag, own, got, out = refs[0], refs[1], refs[2:-1], refs[-1]
    update = own[...]
    for part in got:
        update += part[...].astype(F32)
    out[...] = diag[...] - update


def solution(mesh):
    n_row, n_col = mesh.shape["row"], mesh.shape["col"]

    def on_device(inverse_block, lower_block, pattern, diag_inverse):
        row, col = lax.axis_index("row"), lax.axis_index("col")
        n_j = inverse_block.shape[1]
        rows, cols, b = lower_block.shape[:3]
        masked = mask(pattern, lower_block)

        rounds = line_gather(inverse_block, "col", n_col, 1)

        core = [(i, i ^ 1) for i in range(n_row)]
        pieces = [(masked, row)] + [
            (a, jnp.where(s >= 0, 2 * s + lax.rem(row, 2), -1))
            for got in line_gather(masked, "row", n_row // 2, 2)
            for a, s in got
        ]
        factor = jnp.zeros((n_row,) + masked.shape, BF16)
        for piece, source in pieces:
            other = lax.ppermute(piece, "row", core)
            for value, place in ((piece, source), (other, jnp.where(source >= 0, source ^ 1, -1))):
                there = jnp.maximum(place, 0)
                if n_row > 4:
                    kept = lax.dynamic_index_in_dim(factor, there, 0, keepdims=False)
                    value = jnp.where(place >= 0, value, kept)
                factor = lax.dynamic_update_index_in_dim(factor, value, there, 0)
        factor = factor.reshape((n_col, n_j, cols, b, b))

        early = [(inverse_block, col)] + [x for got in rounds[:-1] for x in got]
        late = rounds[-1]
        total = pl.pallas_call(
            functools.partial(partial_kernel, len(early)),
            out_shape=jax.ShapeDtypeStruct((rows, cols, b, b), F32),
            in_specs=[SMEM] + [VMEM] * (len(early) + 1),
            out_specs=VMEM,
            compiler_params=pltpu.CompilerParams(vmem_limit_bytes=48 << 20),
            cost_estimate=pl.CostEstimate(flops=2 * 24 * b**3, bytes_accessed=4 << 20, transcendentals=0),
        )(jnp.stack([p for _, p in early]).astype(jnp.int32), *[x for x, _ in early], factor)
        piece = jax.ShapeDtypeStruct((cols, b // n_row, b), BF16)
        results = pl.pallas_call(
            functools.partial(finish_kernel, len(late), n_row),
            out_shape=[jax.ShapeDtypeStruct(inverse_block.shape[:1] + lower_block.shape[1:], BF16),
                       jax.ShapeDtypeStruct(piece.shape, F32)] + [piece] * (n_row - 1),
            in_specs=[SMEM] + [VMEM] * (len(late) + 2) + [SMEM, VMEM],
            out_specs=[VMEM] * (n_row + 1),
            scratch_shapes=[pltpu.VMEM((rows, cols, b, b), F32)],
            compiler_params=pltpu.CompilerParams(vmem_limit_bytes=48 << 20),
        )(jnp.stack([p for _, p in late] + [row]).astype(jnp.int32), *[x for x, _ in late],
          factor, total, pattern, masked)
        inverse_lower, own, sends = results[0], results[1], results[2:]
        got = [lax.ppermute(s, "row", [(i, i ^ (d + 1)) for i in range(n_row)]) for d, s in enumerate(sends)]
        inverse_diagonal = pl.pallas_call(
            last_kernel,
            out_shape=jax.ShapeDtypeStruct(diag_inverse.shape, F32),
            in_specs=[VMEM] * (2 + len(got)),
            out_specs=VMEM,
        )(diag_inverse, own, *got)
        return inverse_lower, inverse_diagonal

    blocks, diag = P(("pole", "row"), "col", None, None), P(("pole", "col"), "row", None)
    return jax.shard_map(
        on_device,
        mesh=mesh,
        in_specs=(blocks, blocks, P("row", "col"), diag),
        out_specs=(blocks, diag),
        check_vma=False,
    )
```

```python
import functools

import jax
import jax.numpy as jnp
from jax import lax
from jax.experimental import pallas as pl
from jax.experimental.pallas import tpu as pltpu
from jax.sharding import PartitionSpec as P

F32, BF16 = jnp.float32, jnp.bfloat16
VMEM = pl.BlockSpec(memory_space=pltpu.VMEM)
SMEM = pl.BlockSpec(memory_space=pltpu.SMEM)


def exchange(array, axis, n, distance):
    return lax.ppermute(array, axis, [(i, i ^ distance) for i in range(n)])


def gather(own, axis, n, distances):
    held = [(own, 0)]
    for distance in distances:
        held += [(exchange(a, axis, n, distance), d ^ distance) for a, d in held]
    return held


def column_gather(own, n):
    beside = exchange(own, "col", n, 1)
    held = gather(own, "col", n, [1 << p for p in reversed(range(1, n.bit_length() - 1))])
    beside, *afar = lax.optimization_barrier((beside, *[a for a, _ in held[1:]]))
    afar = [(a, d) for a, (_, d) in zip(afar, held[1:])]
    return [(own, 0), (beside, 1)] + afar + [(exchange(a, "col", n, 1), d ^ 1) for a, d in afar]


def mask_kernel(pattern, token, lower, masked, turned):
    rows, cols = lower.shape[:2]
    for j in range(rows):
        for k in range(cols):
            keep = pattern[j, k].astype(F32)
            value = lower[j, k].astype(F32) * keep
            masked[j, k] = value.astype(BF16)
            turned[j, k] = value.T.astype(BF16)


def add_products(place, block, factor, total):
    rows, inner = block.shape[:2]
    for i in range(rows):
        for k in range(total.shape[1]):
            partial = total[i, k]
            for j in range(inner):
                partial += jnp.dot(block[i, j], factor[place, j, k], preferred_element_type=F32)
            total[i, k] = partial


def early_kernel(n_pieces, n_blocks, owners, places, *refs):
    pieces, blocks, (factor, total) = refs[:n_pieces], refs[n_pieces:n_pieces + n_blocks], refs[n_pieces + n_blocks:]
    for n, piece in enumerate(pieces):
        factor[owners[n]] = piece[...]

    total[...] = jnp.zeros_like(total)
    for n, block in enumerate(blocks):
        add_products(places[n], block, factor, total)


def finish_kernel(n_blocks, n_row, places, *refs):
    blocks = refs[:n_blocks]
    factor, total_in, pattern, turned, lower_out = refs[n_blocks:n_blocks + 5]
    sends, total = refs[n_blocks + 5:-1], refs[-1]
    total[...] = total_in[...]
    for n, block in enumerate(blocks):
        add_products(places[n], block, factor, total)
    row = places[n_blocks]
    rows, cols, b = total.shape[:3]
    piece = b // n_row
    for k in range(cols):
        update = jnp.zeros((b, b), F32)
        for i in range(rows):
            keep = pattern[i, k].astype(F32)
            value = (-(keep * total[i, k])).astype(BF16)
            lower_out[i, k] = value
            update += jnp.dot(turned[i, k], value, preferred_element_type=F32)
        total[0, k] = update
        for d in range(n_row):
            there = pl.multiple_of(jnp.bitwise_xor(row, d) * piece, 16)
            sends[d][k] = total[0, k, pl.ds(there, piece), :].astype(sends[d].dtype)


def last_kernel(*refs):
    diag, own, got, out = refs[0], refs[1], refs[2:-1], refs[-1]
    update = own[...]
    for part in got:
        update += part[...].astype(F32)
    out[...] = diag[...] - update


def call(kernel, out_shape, in_specs, mib, flops=0, scratch=()):
    return pl.pallas_call(
        kernel,
        out_shape=out_shape,
        in_specs=in_specs,
        out_specs=jax.tree.map(lambda _: VMEM, out_shape),
        scratch_shapes=scratch,
        compiler_params=pltpu.CompilerParams(vmem_limit_bytes=mib << 20),
        cost_estimate=pl.CostEstimate(flops=0, bytes_accessed=0, transcendentals=0),
    )


def solution(mesh):
    n_row, n_col = mesh.shape["row"], mesh.shape["col"]

    def on_device(inverse_block, lower_block, pattern, diag_inverse):
        row, col = lax.axis_index("row"), lax.axis_index("col")
        rows, cols, b = lower_block.shape[:3]
        shape = jax.ShapeDtypeStruct

        far = [1 << p for p in range(1, n_row.bit_length() - 1)]
        blocks = column_gather(inverse_block, n_col)
        early, late = blocks[:-1], blocks[-1:]
        token = exchange(pattern, "row", n_row, 1)

        kept = shape(lower_block.shape, BF16)
        masked, turned = call(mask_kernel, [kept, kept], [SMEM, SMEM, VMEM], 60)(pattern, token, lower_block)
        pieces = gather(masked, "row", n_row, far + [1])
        arrays = len(pieces) + len(early)
        factor, total = call(
            functools.partial(early_kernel, len(pieces), len(early)),
            [shape((n_row,) + kept.shape, BF16), shape((rows, cols, b, b), F32)],
            [SMEM, SMEM] + [VMEM] * arrays,
            8 + arrays + n_row,
            48 * b**3,
        )(jnp.stack([row ^ d for _, d in pieces]).astype(jnp.int32), jnp.stack([col ^ d for _, d in early]).astype(jnp.int32),
          *[x for x, _ in pieces], *[x for x, _ in early])
        part = shape((cols, b // n_row, b), BF16)
        lower_out, own, *sends = call(
            functools.partial(finish_kernel, len(late), n_row),
            [shape((rows, cols, b, b), BF16), shape(part.shape, F32)] + [part] * (n_row - 1),
            [SMEM] + [VMEM] * (len(late) + 2) + [SMEM, VMEM],
            12 + n_row,
            24 * b**3,
            [pltpu.VMEM((rows, cols, b, b), F32)],
        )(jnp.stack([col ^ d for _, d in late] + [row]).astype(jnp.int32), *[x for x, _ in late],
          factor, total, pattern, turned)
        got = [exchange(s, "row", n_row, d) for d, s in enumerate(sends, 1)]
        diag_out = call(last_kernel, shape(diag_inverse.shape, F32), [VMEM] * (2 + len(got)), 4)(diag_inverse, own, *got)
        return lower_out, diag_out

    spec, diag = P(("pole", "row"), "col", None, None), P(("pole", "col"), "row", None)
    return jax.shard_map(
        on_device,
        mesh=mesh,
        in_specs=(spec, spec, P("row", "col"), diag),
        out_specs=(spec, diag),
        check_vma=False,
    )
```

```python
import functools

import jax
import jax.numpy as jnp
from jax import lax
from jax.experimental import pallas as pl
from jax.experimental.pallas import tpu as pltpu
from jax.sharding import PartitionSpec as P

F32, BF16 = jnp.float32, jnp.bfloat16
VMEM = pl.BlockSpec(memory_space=pltpu.VMEM)
SMEM = pl.BlockSpec(memory_space=pltpu.SMEM)
ANY = pl.BlockSpec(memory_space=pl.ANY)


def exchange(array, axis, n, distance):
    return lax.ppermute(array, axis, [(i, i ^ distance) for i in range(n)])


def gather(own, axis, n, distances):
    held = [(own, 0)]
    for distance in distances:
        held += [(exchange(a, axis, n, distance), d ^ distance) for a, d in held]
    return held


def column_gather(own, top, bottom, n):
    far = [1 << p for p in reversed(range(1, n.bit_length() - 1))]
    half = top.shape[0]
    beside = exchange(own, "col", n, 1)
    upper = gather(top, "col", n, far)[1:]
    lower = gather(bottom, "col", n, far)[1:]
    arrays, beside = lax.optimization_barrier(([a for a, _ in lower], beside))
    lower = [(a, d) for a, (_, d) in zip(arrays, lower)]
    got = [(0, top, 0), (half, bottom, 0), (0, beside, 1)]
    for start, part in ((0, upper), (half, lower)):
        got += [(start, a, d) for a, d in part]
    upper = [(exchange(a, "col", n, 1), d ^ 1) for a, d in upper]
    afar, arrays = lax.optimization_barrier(([a for a, _ in lower], [a for a, _ in upper]))
    lower = [(a, d) for a, (_, d) in zip(afar, lower)]
    upper = [(a, d) for a, (_, d) in zip(arrays, upper)]
    lower = [(exchange(a, "col", n, 1), d ^ 1) for a, d in lower]
    for start, part in ((0, upper), (half, lower)):
        got += [(start, a, d) for a, d in part]
    return got


def keep(info, cols, i, k):
    return info[2 + i * cols + k].astype(F32)


def mask_kernel(info, token, lower, *masked):
    cols = lower.shape[1]
    for j, out in enumerate(masked):
        for k in range(cols):
            out[k] = (lower[j, k].astype(F32) * keep(info, cols, j, k)).astype(BF16)


def add_products(place, start, block, factor, total):
    rows, inner = block.shape[:2]
    for i in range(rows):
        for k in range(total.shape[1]):
            partial = total[start + i, k]
            for j in range(inner):
                partial += jnp.dot(block[i, j], factor[place, j, k], preferred_element_type=F32)
            total[start + i, k] = partial


def place_kernel(sources, parts, info, *refs):
    n_pieces = len(sources)
    pieces, blocks, (factor, turned, total) = refs[:n_pieces], refs[n_pieces:-3], refs[-3:]
    for (j, d), piece in zip(sources, pieces):
        factor[jnp.bitwise_xor(info[0], d), j] = piece[...]
    for (j, d), piece in zip(sources, pieces):
        if d == 0:
            for k in range(piece.shape[0]):
                turned[j, k] = piece[k].astype(F32).T.astype(BF16)
    total[...] = jnp.zeros_like(total)
    for (start, d), block in zip(parts, blocks):
        add_products(jnp.bitwise_xor(info[1], d), start, block, factor, total)


def early_kernel(parts, info, *refs):
    blocks, (factor, total_in, turned, value, total, update, both) = refs[:-7], refs[-7:]
    rows, cols = total_in.shape[:2]
    half = rows // 2
    both[...] = total_in[...]
    for (start, d), block in zip(parts, blocks):
        add_products(jnp.bitwise_xor(info[1], d), start, block, factor, both)
    for i in range(half, rows):
        total[i - half] = both[i]
    for k in range(cols):
        share = jnp.zeros(update.shape[1:], F32)
        for i in range(half):
            value[i, k] = (-(keep(info, cols, i, k) * both[i, k])).astype(BF16)
            share += jnp.dot(turned[i, k], value[i, k], preferred_element_type=F32)
        update[k] = share


def finish_kernel(n_row, distance, info, block, factor, total, update, turned, value, *refs):
    sends, whole = refs[:-1], refs[-1]
    half, cols, b = total.shape[:3]
    place = jnp.bitwise_xor(info[1], distance)
    piece = b // n_row
    for k in range(cols):
        share = update[k]
        for i in range(half):
            partial = total[i, k]
            for j in range(block.shape[1]):
                partial += jnp.dot(block[i, j], factor[place, j, k], preferred_element_type=F32)
            value[i, k] = (-(keep(info, cols, half + i, k) * partial)).astype(BF16)
            share += jnp.dot(turned[half + i, k], value[i, k], preferred_element_type=F32)
        whole[k] = share
        for d in range(n_row):
            there = pl.multiple_of(jnp.bitwise_xor(info[0], d) * piece, 16)
            sends[d][k] = whole[k, pl.ds(there, piece), :].astype(sends[d].dtype)


def join_kernel(top, bottom, out, sems):
    half = top.shape[0]
    copies = [
        pltpu.make_async_copy(top, out.at[pl.ds(0, half)], sems.at[0]),
        pltpu.make_async_copy(bottom, out.at[pl.ds(half, half)], sems.at[1]),
    ]
    for copy in copies:
        copy.start()
    for copy in copies:
        copy.wait()


def last_kernel(*refs):
    diag, own, got, out = refs[0], refs[1], refs[2:-1], refs[-1]
    update = own[...]
    for part in got:
        update += part[...].astype(F32)
    out[...] = diag[...] - update


def call(kernel, out_shape, in_specs, mib, scratch=(), out_specs=None, aliases={}):
    return pl.pallas_call(
        kernel,
        out_shape=out_shape,
        in_specs=in_specs,
        out_specs=jax.tree.map(lambda _: VMEM, out_shape) if out_specs is None else out_specs,
        scratch_shapes=scratch,
        input_output_aliases=aliases,
        compiler_params=pltpu.CompilerParams(vmem_limit_bytes=mib << 20),
        cost_estimate=pl.CostEstimate(flops=0, bytes_accessed=0, transcendentals=0),
    )


def solution(mesh):
    n_row, n_col = mesh.shape["row"], mesh.shape["col"]

    def on_device(inverse_block, lower_block, pattern, diag_inverse):
        row, col = lax.axis_index("row"), lax.axis_index("col")
        rows, cols, b = lower_block.shape[:3]
        shape = jax.ShapeDtypeStruct

        half = rows // 2
        info = jnp.concatenate([jnp.stack([row, col]).astype(jnp.int32), pattern.reshape(-1)])
        blocks = column_gather(inverse_block, inverse_block[:half], inverse_block[half:], n_col)
        token = exchange(pattern, "row", n_row, 1)

        masked = call(mask_kernel, [shape((cols, b, b), BF16)] * rows, [SMEM, SMEM, VMEM], 4)(info, token, lower_block)
        far = [1 << p for p in range(1, n_row.bit_length() - 1)]
        pieces = [(m, (j, d)) for j, own in enumerate(masked) for m, d in gather(own, "row", n_row, far + [1])]
        near, others, last = [x for x in blocks if x[2] == 0], [x for x in blocks[:-1] if x[2]], blocks[-1]

        kept, ends = shape(lower_block.shape, BF16), shape((half, cols, b, b), F32)
        sums, value = shape((rows, cols, b, b), F32), shape((half, cols, b, b), BF16)
        factor, turned, total = call(
            functools.partial(place_kernel, [x for _, x in pieces], [(start, d) for start, _, d in near]),
            [shape((n_row,) + kept.shape, BF16), kept, sums],
            [SMEM] + [VMEM] * (len(pieces) + len(near)),
            20,
        )(info, *[m for m, _ in pieces], *[x for _, x, _ in near])
        top, total, update = call(
            functools.partial(early_kernel, [(start, d) for start, _, d in others]),
            [value, ends, shape((cols, b, b), F32)],
            [SMEM] + [VMEM] * (len(others) + 3),
            20,
            [pltpu.VMEM(sums.shape, F32)],
        )(info, *[x for _, x, _ in others], factor, total, turned)
        part = shape((cols, b // n_row, b), BF16)
        bottom, own, *sends = call(
            functools.partial(finish_kernel, n_row, last[2]),
            [value, shape(part.shape, F32)] + [part] * (n_row - 1),
            [SMEM] + [VMEM] * 5,
            8,
            [pltpu.VMEM((cols, b, b), F32)],
        )(info, last[1], factor, total, update, turned)
        got = [exchange(s, "row", n_row, d) for d, s in enumerate(sends, 1)]
        lower_out = call(
            join_kernel,
            shape(inverse_block.shape[:1] + lower_block.shape[1:], BF16),
            [VMEM] * 2,
            2,
            [pltpu.SemaphoreType.DMA((2,))],
            ANY,
        )(top, bottom)
        got, lower_out = lax.optimization_barrier((got, lower_out))
        diag_out = call(last_kernel, shape(diag_inverse.shape, F32), [VMEM] * (2 + len(got)), 4)(diag_inverse, own, *got)
        return lower_out, diag_out

    spec, diag = P(("pole", "row"), "col", None, None), P(("pole", "col"), "row", None)
    return jax.shard_map(
        on_device,
        mesh=mesh,
        in_specs=(spec, spec, P("row", "col"), diag),
        out_specs=(spec, diag),
        check_vma=False,
    )
```

```python
import functools

import jax
import jax.numpy as jnp
from jax import lax
from jax.experimental import pallas as pl
from jax.experimental.pallas import tpu as pltpu
from jax.sharding import PartitionSpec as P

F32, BF16 = jnp.float32, jnp.bfloat16
VMEM = pl.BlockSpec(memory_space=pltpu.VMEM)
SMEM = pl.BlockSpec(memory_space=pltpu.SMEM)
ANY = pl.BlockSpec(memory_space=pl.ANY)


def exchange(array, axis, n, distance):
    return lax.ppermute(array, axis, [(i, i ^ distance) for i in range(n)])


def gather(own, axis, n, distances):
    held = [(own, 0)]
    for distance in distances:
        held += [(exchange(a, axis, n, distance), d ^ distance) for a, d in held]
    return held


def column_gather(own, top, bottom, n):
    far = [1 << p for p in reversed(range(1, n.bit_length() - 1))]
    half = top.shape[0]
    beside = exchange(own, "col", n, 1)
    upper = gather(top, "col", n, far)[1:]
    lower = gather(bottom, "col", n, far)[1:]
    arrays, beside = lax.optimization_barrier(([a for a, _ in lower], beside))
    lower = [(a, d) for a, (_, d) in zip(arrays, lower)]
    got = [(0, top, 0), (half, bottom, 0), (0, beside, 1)]
    for start, part in ((0, upper), (half, lower)):
        got += [(start, a, d) for a, d in part]
    upper = [(exchange(a, "col", n, 1), d ^ 1) for a, d in upper]
    afar, arrays = lax.optimization_barrier(([a for a, _ in lower], [a for a, _ in upper]))
    lower = [(a, d) for a, (_, d) in zip(afar, lower)]
    upper = [(a, d) for a, (_, d) in zip(arrays, upper)]
    lower = [(exchange(a, "col", n, 1), d ^ 1) for a, d in lower]
    for start, part in ((0, upper), (half, lower)):
        got += [(start, a, d) for a, d in part]
    return got


def keep(info, cols, i, k):
    return info[2 + i * cols + k].astype(F32)


def mask_kernel(info, token, lower, *masked):
    cols = lower.shape[1]
    for j, out in enumerate(masked):
        for k in range(cols):
            out[k] = (lower[j, k].astype(F32) * keep(info, cols, j, k)).astype(BF16)


def add_products(place, start, block, factor, total):
    rows, inner = block.shape[:2]
    for i in range(rows):
        for k in range(total.shape[1]):
            partial = total[start + i, k]
            for j in range(inner):
                partial += jnp.dot(block[i, j], factor[place, j, k], preferred_element_type=F32)
            total[start + i, k] = partial


def place_kernel(sources, parts, n_row, distance, info, *refs):
    n_pieces = len(sources)
    pieces, blocks, (factor, final, turned, total, whole) = refs[:n_pieces], refs[n_pieces:-5], refs[-5:]
    half, inner, cols, b = final.shape[:4]
    step = b // n_row
    for (j, d), piece in zip(sources, pieces):
        factor[jnp.bitwise_xor(info[0], d), j] = piece[...]
    for i in range(half):
        for j in range(inner):
            for k in range(cols):
                block = factor[jnp.bitwise_xor(info[1], distance), j, k].astype(F32)
                final[i, j, k] = (-keep(info, cols, half + i, k) * block).astype(BF16)
    for (j, d), piece in zip(sources, pieces):
        if d == 0:
            for k in range(cols):
                whole[...] = piece[k].astype(F32).T
                for e in range(n_row):
                    there = pl.multiple_of(jnp.bitwise_xor(info[0], e) * step, 16)
                    turned[j, k, e * step:(e + 1) * step, :] = whole[pl.ds(there, step), :].astype(BF16)
    total[...] = jnp.zeros_like(total)
    for (start, d), block in zip(parts, blocks):
        add_products(jnp.bitwise_xor(info[1], d), start, block, factor, total)


def early_kernel(parts, info, *refs):
    blocks, (factor, total_in, turned, value, total, update, both) = refs[:-7], refs[-7:]
    rows, cols = total_in.shape[:2]
    half = rows // 2
    both[...] = total_in[...]
    for (start, d), block in zip(parts, blocks):
        add_products(jnp.bitwise_xor(info[1], d), start, block, factor, both)
    for k in range(cols):
        share = jnp.zeros(update.shape[1:], F32)
        for i in range(half):
            total[i, k] = -(keep(info, cols, half + i, k) * both[half + i, k])
            value[i, k] = (-(keep(info, cols, i, k) * both[i, k])).astype(BF16)
            share += jnp.dot(turned[i, k], value[i, k], preferred_element_type=F32)
        update[k] = share


def finish_kernel(block, final, total, update, turned, value, *sends):
    half, cols, b = total.shape[:3]
    step = b // len(sends)
    for k in range(cols):
        share = update[k]
        for i in range(half):
            partial = total[i, k]
            for j in range(block.shape[1]):
                partial += jnp.dot(block[i, j], final[i, j, k], preferred_element_type=F32)
            value[i, k] = partial.astype(BF16)
            share += jnp.dot(turned[half + i, k], value[i, k], preferred_element_type=F32)
        for d, send in enumerate(sends):
            send[k] = share[d * step:(d + 1) * step].astype(send.dtype)


def join_kernel(top, bottom, out, sems):
    half = top.shape[0]
    copies = [
        pltpu.make_async_copy(top, out.at[pl.ds(0, half)], sems.at[0]),
        pltpu.make_async_copy(bottom, out.at[pl.ds(half, half)], sems.at[1]),
    ]
    for copy in copies:
        copy.start()
    for copy in copies:
        copy.wait()


def last_kernel(*refs):
    diag, own, got, out = refs[0], refs[1], refs[2:-1], refs[-1]
    update = own[...]
    for part in got:
        update += part[...].astype(F32)
    out[...] = diag[...] - update


def call(kernel, out_shape, in_specs, mib, scratch=(), out_specs=None, aliases={}):
    return pl.pallas_call(
        kernel,
        out_shape=out_shape,
        in_specs=in_specs,
        out_specs=jax.tree.map(lambda _: VMEM, out_shape) if out_specs is None else out_specs,
        scratch_shapes=scratch,
        input_output_aliases=aliases,
        compiler_params=pltpu.CompilerParams(vmem_limit_bytes=mib << 20),
        cost_estimate=pl.CostEstimate(flops=0, bytes_accessed=0, transcendentals=0),
    )


def solution(mesh):
    n_row, n_col = mesh.shape["row"], mesh.shape["col"]

    def on_device(inverse_block, lower_block, pattern, diag_inverse):
        row, col = lax.axis_index("row"), lax.axis_index("col")
        rows, cols, b = lower_block.shape[:3]
        shape = jax.ShapeDtypeStruct

        half = rows // 2
        info = jnp.concatenate([jnp.stack([row, col]).astype(jnp.int32), pattern.reshape(-1)])
        blocks = column_gather(inverse_block, inverse_block[:half], inverse_block[half:], n_col)
        token = exchange(pattern, "row", n_row, 1)

        masked = call(mask_kernel, [shape((cols, b, b), BF16)] * rows, [SMEM, SMEM, VMEM], 4)(info, token, lower_block)
        far = [1 << p for p in range(1, n_row.bit_length() - 1)]
        pieces = [(m, (j, d)) for j, own in enumerate(masked) for m, d in gather(own, "row", n_row, far + [1])]
        near, others, last = [x for x in blocks if x[2] == 0], [x for x in blocks[:-1] if x[2]], blocks[-1]

        kept, ends = shape(lower_block.shape, BF16), shape((half, cols, b, b), F32)
        sums, value = shape((rows, cols, b, b), F32), shape((half, cols, b, b), BF16)
        final = shape((half,) + last[1].shape[1:2] + (cols, b, b), BF16)
        factor, final, turned, total = call(
            functools.partial(place_kernel, [x for _, x in pieces], [(start, d) for start, _, d in near], n_row, last[2]),
            [shape((n_row,) + kept.shape, BF16), final, kept, sums],
            [SMEM] + [VMEM] * (len(pieces) + len(near)),
            20,
            [pltpu.VMEM((b, b), F32)],
        )(info, *[m for m, _ in pieces], *[x for _, x, _ in near])
        top, total, update = call(
            functools.partial(early_kernel, [(start, d) for start, _, d in others]),
            [value, ends, shape((cols, b, b), F32)],
            [SMEM] + [VMEM] * (len(others) + 3),
            20,
            [pltpu.VMEM(sums.shape, F32)],
        )(info, *[x for _, x, _ in others], factor, total, turned)
        part = shape((cols, b // n_row, b), BF16)
        bottom, own, *sends = call(
            finish_kernel,
            [value, shape(part.shape, F32)] + [part] * (n_row - 1),
            [VMEM] * 5,
            8,
        )(last[1], final, total, update, turned)
        lower_out = call(
            join_kernel,
            shape(inverse_block.shape[:1] + lower_block.shape[1:], BF16),
            [VMEM] * 2,
            2,
            [pltpu.SemaphoreType.DMA((2,))],
            ANY,
        )(top, bottom)
        got = [exchange(s, "row", n_row, d) for d, s in enumerate(sends, 1)]
        got, lower_out = lax.optimization_barrier((got, lower_out))
        diag_out = call(last_kernel, shape(diag_inverse.shape, F32), [VMEM] * (2 + len(got)), 4)(diag_inverse, own, *got)
        return lower_out, diag_out

    spec, diag = P(("pole", "row"), "col", None, None), P(("pole", "col"), "row", None)
    return jax.shard_map(
        on_device,
        mesh=mesh,
        in_specs=(spec, spec, P("row", "col"), diag),
        out_specs=(spec, diag),
        check_vma=False,
    )
```

```python
import functools

import jax
import jax.numpy as jnp
from jax import lax
from jax.experimental import pallas as pl
from jax.experimental.pallas import tpu as pltpu
from jax.sharding import PartitionSpec as P

F32, BF16 = jnp.float32, jnp.bfloat16
VMEM = pl.BlockSpec(memory_space=pltpu.VMEM)
SMEM = pl.BlockSpec(memory_space=pltpu.SMEM)
ANY = pl.BlockSpec(memory_space=pl.ANY)


def exchange(array, axis, n, distance):
    return lax.ppermute(array, axis, [(i, i ^ distance) for i in range(n)])


def gather(own, axis, n, distances):
    held = [(own, 0)]
    for distance in distances:
        held += [(exchange(a, axis, n, distance), d ^ distance) for a, d in held]
    return held


def column_gather(own, n, cut):
    far = [1 << p for p in reversed(range(1, n.bit_length() - 1))]
    whole, first, rest = slice(0, own.shape[2]), slice(0, cut), slice(cut, own.shape[2])
    beside = exchange(own, "col", n, 1)
    upper = gather(own[:, :, first], "col", n, far)[1:]
    lower = gather(own[:, :, rest], "col", n, far)[1:]
    arrays, beside = lax.optimization_barrier(([a for a, _ in lower], beside))
    lower = [(a, d) for a, (_, d) in zip(arrays, lower)]
    top = [(exchange(a, "col", n, 1), d ^ 1) for a, d in upper]
    arrays, before = lax.optimization_barrier(([a for a, _ in lower], [a for a, _ in top]))
    lower = [(a, d) for a, (_, d) in zip(arrays, lower)]
    top = [(a, d) for a, (_, d) in zip(before, top)]
    late = [(rest, exchange(a, "col", n, 1), d ^ 1) for a, d in lower]
    early = [(whole, own, 0), (whole, beside, 1)] + [(first, a, d) for a, d in upper] + [(rest, a, d) for a, d in lower]
    return early + [(first, a, d) for a, d in top], late


def keep(info, cols, i, k):
    return info[2 + i * cols + k].astype(F32)


def mask_kernel(info, token, lower, *masked):
    cols = lower.shape[1]
    for j, out in enumerate(masked):
        for k in range(cols):
            out[k] = (lower[j, k].astype(F32) * keep(info, cols, j, k)).astype(BF16)


def early_kernel(sources, parts, n_row, distance, info, *refs):
    n_pieces = len(sources)
    pieces, blocks, (final, turned, total, factor, whole) = refs[:n_pieces], refs[n_pieces:-5], refs[-5:]
    rows, inner, cols, b = final.shape[:4]
    step = b // n_row
    for (j, d), piece in zip(sources, pieces):
        factor[jnp.bitwise_xor(info[0], d), j] = piece[...]
    for i in range(rows):
        for k in range(cols):
            sign = -keep(info, cols, i, k)
            for j in range(inner):
                final[i, j, k] = (sign * factor[jnp.bitwise_xor(info[1], distance), j, k].astype(F32)).astype(BF16)
            whole[...] = pieces[sources.index((i, 0))][k].astype(F32).T
            for d in range(n_row):
                there = pl.multiple_of(jnp.bitwise_xor(info[0], d) * step, 16)
                turned[i, k, d * step:(d + 1) * step, :] = whole[pl.ds(there, step), :].astype(BF16)
            total[i, k] = jnp.zeros((b, b), F32)
            for (at, d), block in zip(parts, blocks):
                partial = total[i, k, at, :]
                for j in range(inner):
                    partial += jnp.dot(
                        block[i, j], factor[jnp.bitwise_xor(info[1], d), j, k], preferred_element_type=F32
                    )
                total[i, k, at, :] = partial
            total[i, k] = sign * total[i, k]


def finish_kernel(parts, *refs):
    blocks, (final, total, turned, value, kept, sent) = refs[:len(parts)], refs[len(parts):]
    rows, cols, b = total.shape[:3]
    step = kept.shape[2]
    start = parts[0].start
    for k in range(cols):
        share = jnp.zeros((b, b), F32)
        for i in range(rows):
            value[i, k, :start, :] = total[i, k, :start, :].astype(BF16)
            for at, block in zip(parts, blocks):
                partial = total[i, k, at, :]
                for j in range(block.shape[1]):
                    partial += jnp.dot(block[i, j], final[i, j, k], preferred_element_type=F32)
                value[i, k, at, :] = partial.astype(BF16)
            share += jnp.dot(turned[i, k], value[i, k], preferred_element_type=F32)
        for m in range(kept.shape[0]):
            at = 2 * m * step
            kept[m, k] = share[at:at + step]
            sent[m, k] = share[at + step:at + 2 * step].astype(BF16)


def chip_kernel(kept, got, own, *sends):
    own[...] = kept[0] + got[0].astype(F32)
    for m, send in enumerate(sends, 1):
        send[...] = (kept[m] + got[m].astype(F32)).astype(BF16)


def join_kernel(value, out, sem):
    copy = pltpu.make_async_copy(value, out, sem)
    copy.start()
    copy.wait()


def last_kernel(*refs):
    diag, own, got, out = refs[0], refs[1], refs[2:-1], refs[-1]
    update = own[...]
    for part in got:
        update += part[...].astype(F32)
    out[...] = diag[...] - update


def call(kernel, out_shape, in_specs, mib, scratch=(), out_specs=None, aliases={}):
    return pl.pallas_call(
        kernel,
        out_shape=out_shape,
        in_specs=in_specs,
        out_specs=jax.tree.map(lambda _: VMEM, out_shape) if out_specs is None else out_specs,
        scratch_shapes=scratch,
        input_output_aliases=aliases,
        compiler_params=pltpu.CompilerParams(vmem_limit_bytes=mib << 20),
        cost_estimate=pl.CostEstimate(flops=0, bytes_accessed=0, transcendentals=0),
    )


def solution(mesh):
    n_row, n_col = mesh.shape["row"], mesh.shape["col"]

    def on_device(inverse_block, lower_block, pattern, diag_inverse):
        row, col = lax.axis_index("row"), lax.axis_index("col")
        rows, cols, b = lower_block.shape[:3]
        shape = jax.ShapeDtypeStruct

        info = jnp.concatenate([jnp.stack([row, col]).astype(jnp.int32), pattern.reshape(-1)])
        early, late = column_gather(inverse_block, n_col, inverse_block.shape[2] * 7 // 16)
        token = exchange(pattern, "row", n_row, 1)

        kept = shape(lower_block.shape, BF16)
        masked = call(mask_kernel, [shape((cols, b, b), BF16)] * rows, [SMEM, SMEM, VMEM], 4)(info, token, lower_block)
        order = [1 << p for p in range(1, n_row.bit_length() - 1)] + [1]
        pieces = [(m, (j, d)) for j, own in enumerate(masked) for m, d in gather(own, "row", n_row, order)]
        last, early = late[-1:], early + late[:-1]

        sums = shape((rows, cols, b, b), F32)
        final, turned, total = call(
            functools.partial(
                early_kernel, [d for _, d in pieces], [(at, d) for at, _, d in early], n_row, last[0][2]
            ),
            [shape((rows,) + inverse_block.shape[1:2] + kept.shape[1:], BF16), kept, sums],
            [SMEM] + [VMEM] * (len(pieces) + len(early)),
            16 + n_row,
            [pltpu.VMEM((n_row,) + kept.shape, BF16), pltpu.VMEM((b, b), F32)],
        )(info, *[m for m, _ in pieces], *[x for _, x, _ in early])
        part = shape((cols, b // n_row, b), BF16)
        pairs = (n_row // 2,) + part.shape
        value, mine, theirs = call(
            functools.partial(finish_kernel, [at for at, _, _ in last]),
            [shape(sums.shape, BF16), shape(pairs, F32), shape(pairs, BF16)],
            [VMEM] * (len(last) + 3),
            8,
        )(*[x for _, x, _ in last], final, total, turned)
        own, *sends = call(chip_kernel, [shape(part.shape, F32)] + [part] * (n_row // 2 - 1), [VMEM] * 2, 2)(
            mine, exchange(theirs, "row", n_row, 1)
        )
        lower_out = call(
            join_kernel,
            shape(sums.shape, BF16),
            [VMEM],
            2,
            [pltpu.SemaphoreType.DMA(())],
            ANY,
        )(value)
        got = [exchange(s, "row", n_row, 2 * m) for m, s in enumerate(sends, 1)]
        got, lower_out = lax.optimization_barrier((got, lower_out))
        diag_out = call(last_kernel, shape(diag_inverse.shape, F32), [VMEM] * (2 + len(got)), 4)(diag_inverse, own, *got)
        return lower_out, diag_out

    spec, diag = P(("pole", "row"), "col", None, None), P(("pole", "col"), "row", None)
    return jax.shard_map(
        on_device,
        mesh=mesh,
        in_specs=(spec, spec, P("row", "col"), diag),
        out_specs=(spec, diag),
        check_vma=False,
    )
```

```python
import functools

import jax
import jax.numpy as jnp
from jax import lax
from jax.experimental import pallas as pl
from jax.experimental.pallas import tpu as pltpu
from jax.sharding import PartitionSpec as P

F32, BF16 = jnp.float32, jnp.bfloat16
VMEM = pl.BlockSpec(memory_space=pltpu.VMEM)
SMEM = pl.BlockSpec(memory_space=pltpu.SMEM)
ANY = pl.BlockSpec(memory_space=pl.ANY)


def exchange(array, axis, n, distance):
    return lax.ppermute(array, axis, [(i, i ^ distance) for i in range(n)])


def gather(own, axis, n, distances):
    held = [(own, 0)]
    for distance in distances:
        held += [(exchange(a, axis, n, distance), d ^ distance) for a, d in held]
    return held


def cut_kernel(whole, first, rest):
    first[...] = whole[:, :, :first.shape[2], :]
    rest[...] = whole[:, :, first.shape[2]:, :]


def cut_rows(whole, cut):
    i, j, a, b = whole.shape
    return call(
        cut_kernel,
        [jax.ShapeDtypeStruct((i, j, cut, b), BF16), jax.ShapeDtypeStruct((i, j, a - cut, b), BF16)],
        [VMEM],
        4,
    )(whole)


def column_gather(own, n, cut):
    far = [1 << p for p in reversed(range(1, n.bit_length() - 1))]
    whole, first, rest = slice(0, own.shape[2]), slice(0, cut), slice(cut, own.shape[2])
    head, tail = cut_rows(own, cut)
    beside = exchange(own, "col", n, 1)
    upper = gather(head, "col", n, far)[1:]
    lower = gather(tail, "col", n, far)[1:]
    arrays, beside = lax.optimization_barrier(([a for a, _ in lower], beside))
    lower = [(a, d) for a, (_, d) in zip(arrays, lower)]
    top = [(exchange(a, "col", n, 1), d ^ 1) for a, d in upper]
    arrays, before = lax.optimization_barrier(([a for a, _ in lower], [a for a, _ in top]))
    lower = [(a, d) for a, (_, d) in zip(arrays, lower)]
    top = [(a, d) for a, (_, d) in zip(before, top)]
    late = [(rest, exchange(a, "col", n, 1), d ^ 1) for a, d in lower]
    early = [(whole, own, 0), (whole, beside, 1)] + [(first, a, d) for a, d in upper] + [(rest, a, d) for a, d in lower]
    return early + [(first, a, d) for a, d in top], late


def keep(info, cols, i, k):
    return info[2 + i * cols + k].astype(F32)


def mask_kernel(info, token, lower, *masked):
    cols = lower.shape[1]
    for j, out in enumerate(masked):
        for k in range(cols):
            out[k] = (lower[j, k].astype(F32) * keep(info, cols, j, k)).astype(BF16)


def early_kernel(sources, parts, n_row, distance, info, *refs):
    n_pieces = len(sources)
    pieces, blocks, (final, turned, total, factor, whole) = refs[:n_pieces], refs[n_pieces:-5], refs[-5:]
    rows, inner, cols, b = final.shape[:4]
    step = b // n_row
    for (j, d), piece in zip(sources, pieces):
        factor[jnp.bitwise_xor(info[0], d), j] = piece[...]
    for i in range(rows):
        for k in range(cols):
            sign = -keep(info, cols, i, k)
            for j in range(inner):
                final[i, j, k] = (sign * factor[jnp.bitwise_xor(info[1], distance), j, k].astype(F32)).astype(BF16)
            whole[...] = pieces[sources.index((i, 0))][k].astype(F32).T
            for d in range(n_row):
                there = pl.multiple_of(jnp.bitwise_xor(info[0], d) * step, 16)
                turned[i, k, d * step:(d + 1) * step, :] = whole[pl.ds(there, step), :].astype(BF16)
            total[i, k] = jnp.zeros((b, b), F32)
            for (at, d), block in zip(parts, blocks):
                partial = total[i, k, at, :]
                for j in range(inner):
                    partial += jnp.dot(
                        block[i, j], factor[jnp.bitwise_xor(info[1], d), j, k], preferred_element_type=F32
                    )
                total[i, k, at, :] = partial
            total[i, k] = sign * total[i, k]


def finish_kernel(parts, *refs):
    blocks, (final, total, turned, value, kept, sent) = refs[:len(parts)], refs[len(parts):]
    rows, cols, b = total.shape[:3]
    step = kept.shape[2]
    start = parts[0].start
    for k in range(cols):
        share = jnp.zeros((b, b), F32)
        for i in range(rows):
            value[i, k, :start, :] = total[i, k, :start, :].astype(BF16)
            for at, block in zip(parts, blocks):
                partial = total[i, k, at, :]
                for j in range(block.shape[1]):
                    partial += jnp.dot(block[i, j], final[i, j, k], preferred_element_type=F32)
                value[i, k, at, :] = partial.astype(BF16)
            share += jnp.dot(turned[i, k], value[i, k], preferred_element_type=F32)
        for m in range(kept.shape[0]):
            at = 2 * m * step
            kept[m, k] = share[at:at + step]
            sent[m, k] = share[at + step:at + 2 * step].astype(BF16)


def chip_kernel(kept, got, own, *sends):
    own[...] = kept[0] + got[0].astype(F32)
    for m, send in enumerate(sends, 1):
        send[...] = (kept[m] + got[m].astype(F32)).astype(BF16)


def join_kernel(value, out, sem):
    copy = pltpu.make_async_copy(value, out, sem)
    copy.start()
    copy.wait()


def last_kernel(*refs):
    diag, own, got, out = refs[0], refs[1], refs[2:-1], refs[-1]
    update = own[...]
    for part in got:
        update += part[...].astype(F32)
    out[...] = diag[...] - update


def call(kernel, out_shape, in_specs, mib, scratch=(), out_specs=None, aliases={}):
    return pl.pallas_call(
        kernel,
        out_shape=out_shape,
        in_specs=in_specs,
        out_specs=jax.tree.map(lambda _: VMEM, out_shape) if out_specs is None else out_specs,
        scratch_shapes=scratch,
        input_output_aliases=aliases,
        compiler_params=pltpu.CompilerParams(vmem_limit_bytes=mib << 20),
        cost_estimate=pl.CostEstimate(flops=0, bytes_accessed=0, transcendentals=0),
    )


def solution(mesh):
    n_row, n_col = mesh.shape["row"], mesh.shape["col"]

    def on_device(inverse_block, lower_block, pattern, diag_inverse):
        row, col = lax.axis_index("row"), lax.axis_index("col")
        rows, cols, b = lower_block.shape[:3]
        shape = jax.ShapeDtypeStruct

        info = jnp.concatenate([jnp.stack([row, col]).astype(jnp.int32), pattern.reshape(-1)])
        early, late = column_gather(inverse_block, n_col, inverse_block.shape[2] * 7 // 16)
        token = exchange(pattern, "row", n_row, 1)

        kept = shape(lower_block.shape, BF16)
        masked = call(mask_kernel, [shape((cols, b, b), BF16)] * rows, [SMEM, SMEM, VMEM], 4)(info, token, lower_block)
        order = [1 << p for p in range(1, n_row.bit_length() - 1)] + [1]
        pieces = [(m, (j, d)) for j, own in enumerate(masked) for m, d in gather(own, "row", n_row, order)]
        last, early = late[-1:], early + late[:-1]

        sums = shape((rows, cols, b, b), F32)
        final, turned, total = call(
            functools.partial(
                early_kernel, [d for _, d in pieces], [(at, d) for at, _, d in early], n_row, last[0][2]
            ),
            [shape((rows,) + inverse_block.shape[1:2] + kept.shape[1:], BF16), kept, sums],
            [SMEM] + [VMEM] * (len(pieces) + len(early)),
            16 + n_row,
            [pltpu.VMEM((n_row,) + kept.shape, BF16), pltpu.VMEM((b, b), F32)],
        )(info, *[m for m, _ in pieces], *[x for _, x, _ in early])
        part = shape((cols, b // n_row, b), BF16)
        pairs = (n_row // 2,) + part.shape
        value, mine, theirs = call(
            functools.partial(finish_kernel, [at for at, _, _ in last]),
            [shape(sums.shape, BF16), shape(pairs, F32), shape(pairs, BF16)],
            [VMEM] * (len(last) + 3),
            8,
        )(*[x for _, x, _ in last], final, total, turned)
        own, *sends = call(chip_kernel, [shape(part.shape, F32)] + [part] * (n_row // 2 - 1), [VMEM] * 2, 2)(
            mine, exchange(theirs, "row", n_row, 1)
        )
        lower_out = call(
            join_kernel,
            shape(sums.shape, BF16),
            [VMEM],
            2,
            [pltpu.SemaphoreType.DMA(())],
            ANY,
        )(value)
        got = [exchange(s, "row", n_row, 2 * m) for m, s in enumerate(sends, 1)]
        got, lower_out = lax.optimization_barrier((got, lower_out))
        diag_out = call(last_kernel, shape(diag_inverse.shape, F32), [VMEM] * (2 + len(got)), 4)(diag_inverse, own, *got)
        return lower_out, diag_out

    spec, diag = P(("pole", "row"), "col", None, None), P(("pole", "col"), "row", None)
    return jax.shard_map(
        on_device,
        mesh=mesh,
        in_specs=(spec, spec, P("row", "col"), diag),
        out_specs=(spec, diag),
        check_vma=False,
    )
```

```python
import functools

import jax
import jax.numpy as jnp
from jax import lax
from jax.experimental import pallas as pl
from jax.experimental.pallas import tpu as pltpu
from jax.sharding import PartitionSpec as P

F32, BF16 = jnp.float32, jnp.bfloat16
VMEM = pl.BlockSpec(memory_space=pltpu.VMEM)
SMEM = pl.BlockSpec(memory_space=pltpu.SMEM)
ANY = pl.BlockSpec(memory_space=pl.ANY)


def exchange(array, axis, n, distance):
    return lax.ppermute(array, axis, [(i, i ^ distance) for i in range(n)])


def gather(own, axis, n, distances):
    held = [(own, 0)]
    for distance in distances:
        held += [(exchange(a, axis, n, distance), d ^ distance) for a, d in held]
    return held


def column_gather(own, top, bottom, n):
    far = [1 << p for p in reversed(range(1, n.bit_length() - 1))]
    half = top.shape[0]
    beside = exchange(own, "col", n, 1)
    upper = gather(top, "col", n, far)[1:]
    lower = gather(bottom, "col", n, far)[1:]
    arrays, beside = lax.optimization_barrier(([a for a, _ in lower], beside))
    lower = [(a, d) for a, (_, d) in zip(arrays, lower)]
    got = [(0, top, 0), (half, bottom, 0), (0, beside, 1)]
    for start, part in ((0, upper), (half, lower)):
        got += [(start, a, d) for a, d in part]
    upper = [(exchange(a, "col", n, 1), d ^ 1) for a, d in upper]
    afar, arrays = lax.optimization_barrier(([a for a, _ in lower], [a for a, _ in upper]))
    lower = [(a, d) for a, (_, d) in zip(afar, lower)]
    upper = [(a, d) for a, (_, d) in zip(arrays, upper)]
    lower = [(exchange(a, "col", n, 1), d ^ 1) for a, d in lower]
    for start, part in ((0, upper), (half, lower)):
        got += [(start, a, d) for a, d in part]
    return got


def keep(info, cols, i, k):
    return info[2 + i * cols + k].astype(F32)


def mask_kernel(info, token, lower, *masked):
    cols = lower.shape[1]
    for j, out in enumerate(masked):
        for k in range(cols):
            out[k] = (lower[j, k].astype(F32) * keep(info, cols, j, k)).astype(BF16)


def add_products(place, start, block, factor, total):
    rows, inner = block.shape[:2]
    for i in range(rows):
        for k in range(total.shape[1]):
            partial = total[start + i, k]
            for j in range(inner):
                partial += jnp.dot(block[i, j], factor[place, j, k], preferred_element_type=F32)
            total[start + i, k] = partial


def place_kernel(sources, parts, n_row, distance, info, *refs):
    n_pieces = len(sources)
    pieces, blocks, (factor, final, turned, total, whole) = refs[:n_pieces], refs[n_pieces:-5], refs[-5:]
    half, inner, cols, b = final.shape[:4]
    step = b // n_row
    for (j, d), piece in zip(sources, pieces):
        factor[jnp.bitwise_xor(info[0], d), j] = piece[...]
    for i in range(half):
        for j in range(inner):
            for k in range(cols):
                block = factor[jnp.bitwise_xor(info[1], distance), j, k].astype(F32)
                final[i, j, k] = (-keep(info, cols, half + i, k) * block).astype(BF16)
    for (j, d), piece in zip(sources, pieces):
        if d == 0:
            for k in range(cols):
                whole[...] = piece[k].astype(F32).T
                for e in range(n_row):
                    there = pl.multiple_of(jnp.bitwise_xor(info[0], e) * step, 16)
                    turned[j, k, e * step:(e + 1) * step, :] = whole[pl.ds(there, step), :].astype(BF16)
    total[...] = jnp.zeros_like(total)
    for (start, d), block in zip(parts, blocks):
        add_products(jnp.bitwise_xor(info[1], d), start, block, factor, total)


def early_kernel(parts, info, *refs):
    blocks, (factor, total_in, turned, value, total, update, both) = refs[:-7], refs[-7:]
    rows, cols = total_in.shape[:2]
    half = rows // 2
    both[...] = total_in[...]
    for (start, d), block in zip(parts, blocks):
        add_products(jnp.bitwise_xor(info[1], d), start, block, factor, both)
    for k in range(cols):
        share = jnp.zeros(update.shape[1:], F32)
        for i in range(half):
            total[i, k] = -(keep(info, cols, half + i, k) * both[half + i, k])
            value[i, k] = (-(keep(info, cols, i, k) * both[i, k])).astype(BF16)
            share += jnp.dot(turned[i, k], value[i, k], preferred_element_type=F32)
        update[k] = share


def finish_kernel(block, final, total, update, turned, value, kept, sent):
    half, cols, b = total.shape[:3]
    step = kept.shape[2]
    for k in range(cols):
        share = update[k]
        for i in range(half):
            partial = total[i, k]
            for j in range(block.shape[1]):
                partial += jnp.dot(block[i, j], final[i, j, k], preferred_element_type=F32)
            value[i, k] = partial.astype(BF16)
            share += jnp.dot(turned[half + i, k], value[i, k], preferred_element_type=F32)
        for m in range(kept.shape[0]):
            at = 2 * m * step
            kept[m, k] = share[at:at + step]
            sent[m, k] = share[at + step:at + 2 * step].astype(BF16)


def chip_kernel(kept, got, own, *sends):
    own[...] = kept[0] + got[0].astype(F32)
    for m, send in enumerate(sends, 1):
        send[...] = (kept[m] + got[m].astype(F32)).astype(BF16)


def join_kernel(top, bottom, out, sems):
    half = top.shape[0]
    copies = [
        pltpu.make_async_copy(top, out.at[pl.ds(0, half)], sems.at[0]),
        pltpu.make_async_copy(bottom, out.at[pl.ds(half, half)], sems.at[1]),
    ]
    for copy in copies:
        copy.start()
    for copy in copies:
        copy.wait()


def last_kernel(*refs):
    diag, own, got, out = refs[0], refs[1], refs[2:-1], refs[-1]
    update = own[...]
    for part in got:
        update += part[...].astype(F32)
    out[...] = diag[...] - update


def call(kernel, out_shape, in_specs, mib, scratch=(), out_specs=None, aliases={}):
    return pl.pallas_call(
        kernel,
        out_shape=out_shape,
        in_specs=in_specs,
        out_specs=jax.tree.map(lambda _: VMEM, out_shape) if out_specs is None else out_specs,
        scratch_shapes=scratch,
        input_output_aliases=aliases,
        compiler_params=pltpu.CompilerParams(vmem_limit_bytes=mib << 20),
        cost_estimate=pl.CostEstimate(flops=0, bytes_accessed=0, transcendentals=0),
    )


def solution(mesh):
    n_row, n_col = mesh.shape["row"], mesh.shape["col"]

    def on_device(inverse_block, lower_block, pattern, diag_inverse):
        row, col = lax.axis_index("row"), lax.axis_index("col")
        rows, cols, b = lower_block.shape[:3]
        shape = jax.ShapeDtypeStruct

        half = rows // 2
        info = jnp.concatenate([jnp.stack([row, col]).astype(jnp.int32), pattern.reshape(-1)])
        blocks = column_gather(inverse_block, inverse_block[:half], inverse_block[half:], n_col)
        token = exchange(pattern, "row", n_row, 1)

        masked = call(mask_kernel, [shape((cols, b, b), BF16)] * rows, [SMEM, SMEM, VMEM], 4)(info, token, lower_block)
        far = [1 << p for p in range(1, n_row.bit_length() - 1)]
        pieces = [(m, (j, d)) for j, own in enumerate(masked) for m, d in gather(own, "row", n_row, far + [1])]
        near, others, last = [x for x in blocks if x[2] == 0], [x for x in blocks[:-1] if x[2]], blocks[-1]

        kept, ends = shape(lower_block.shape, BF16), shape((half, cols, b, b), F32)
        sums, value = shape((rows, cols, b, b), F32), shape((half, cols, b, b), BF16)
        final = shape((half,) + last[1].shape[1:2] + (cols, b, b), BF16)
        factor, final, turned, total = call(
            functools.partial(place_kernel, [x for _, x in pieces], [(start, d) for start, _, d in near], n_row, last[2]),
            [shape((n_row,) + kept.shape, BF16), final, kept, sums],
            [SMEM] + [VMEM] * (len(pieces) + len(near)),
            20,
            [pltpu.VMEM((b, b), F32)],
        )(info, *[m for m, _ in pieces], *[x for _, x, _ in near])
        top, total, update = call(
            functools.partial(early_kernel, [(start, d) for start, _, d in others]),
            [value, ends, shape((cols, b, b), F32)],
            [SMEM] + [VMEM] * (len(others) + 3),
            20,
            [pltpu.VMEM(sums.shape, F32)],
        )(info, *[x for _, x, _ in others], factor, total, turned)
        part = shape((cols, b // n_row, b), BF16)
        pairs = (n_row // 2,) + part.shape
        bottom, mine, theirs = call(
            finish_kernel,
            [value, shape(pairs, F32), shape(pairs, BF16)],
            [VMEM] * 5,
            8,
        )(last[1], final, total, update, turned)
        own, *sends = call(chip_kernel, [shape(part.shape, F32)] + [part] * (n_row // 2 - 1), [VMEM] * 2, 2)(
            mine, exchange(theirs, "row", n_row, 1)
        )
        lower_out = call(
            join_kernel,
            shape(inverse_block.shape[:1] + lower_block.shape[1:], BF16),
            [VMEM] * 2,
            2,
            [pltpu.SemaphoreType.DMA((2,))],
            ANY,
        )(top, bottom)
        got = [exchange(s, "row", n_row, 2 * m) for m, s in enumerate(sends, 1)]
        got, lower_out = lax.optimization_barrier((got, lower_out))
        diag_out = call(last_kernel, shape(diag_inverse.shape, F32), [VMEM] * (2 + len(got)), 4)(diag_inverse, own, *got)
        return lower_out, diag_out

    spec, diag = P(("pole", "row"), "col", None, None), P(("pole", "col"), "row", None)
    return jax.shard_map(
        on_device,
        mesh=mesh,
        in_specs=(spec, spec, P("row", "col"), diag),
        out_specs=(spec, diag),
        check_vma=False,
    )
```
